32 devices in a mesh: dp: 8 (over z, y), group: 4 (over x, core).
Axes of the slice: x: 2, y: 2, z: 4, core: 2. Of those that a mesh axis runs over, the one named last changes fastest.
Arguments:
- queries: bfloat16 [4096, 2048], P(('dp', 'group')), may hold values from -100 to 100
- key_states: bfloat16 [4096, 512], P(('dp', 'group')), may hold values from -4 to 4
- value_states: bfloat16 [4096, 512], P(('dp', 'group')), may hold values from -6 to 6
- grad_out: bfloat16 [4096, 2048], P(('dp', 'group')), may hold values from -6 to 6
- doc_ids: int32 [4096], P(('dp', 'group')), may hold values from 0 to 5, never falling along the last dimension, each value on 1 to 896 neighbouring positions
Outputs:
- attended: bfloat16 [4096, 2048], P(('dp', 'group'))
- grad_queries: bfloat16 [4096, 2048], P(('dp', 'group'))
- grad_keys: bfloat16 [4096, 512], P(('dp', 'group'))
- grad_values: bfloat16 [4096, 512], P(('dp', 'group'))
The draws below stay inside these ranges and needn't reach their ends.
Inputs may be any that keep to these rules, and one draw needn't show every extreme that they name: `doc_ids`: ids never fall along the window; every document holds 1 to 896 tokens, and some document exactly 896.
All inputs are finite; a program needn't handle non-finite values.
Results may differ from the reference program's by a relative error of at most 0.02.
Values may be sent and summed in bfloat16 or wider, within the bound.
No kernel may reach another device: no remote copies, remote signals or barrier semaphores. Data moves between devices by JAX's collectives and lax.ppermute only.
A program may use at most 64 MiB of HBM per device.

```python
import math
import jax
import jax.numpy as jnp
import numpy as np
from jax import lax

HEADS = 16
KV_HEADS = 4
HEAD = 128
TOK_DEV = 128
WINDOW = 8
TOKENS = 4096
MAXDOC = 896
NDOCS = 6


def key_field(key):
    base = jax.random.normal(jax.random.fold_in(key, 7), (TOKENS, KV_HEADS * HEAD), jnp.float32)
    return jnp.clip(base, -4.0, 4.0)


def draw_key_states(key, part):
    return key_field(key).astype(jnp.bfloat16)


def draw_queries(key, part):
    drawn = jax.random.normal(jax.random.fold_in(key, 13), (TOKENS, HEADS * HEAD), jnp.float32)
    drawn = jnp.clip(drawn, -4.0, 4.0)
    return drawn.astype(jnp.bfloat16)


def shard_levels(own_key, extent, split, least, largest):
    loudness, own = 1.0, jax.random.fold_in(own_key, 6)
    for dim, parts in split:
        steps = jnp.exp(jax.random.uniform(jax.random.fold_in(own, dim), (parts,), jnp.float32, least / len(split), largest / len(split)))
        loudness = loudness * jnp.repeat(steps, extent[dim] // parts).reshape([-1 if axis == dim else 1 for axis in range(len(extent))])
    return loudness


def split_up(count, total, reach, skew):
    portions = [(1 << 20) // math.isqrt(grade ** skew) + 1 for grade in range(2, count + 1)]
    spare, counts = total - reach - (count - 1), [1] * (count - 1)
    while spare > 0:
        movable = [i for i in range(count - 1) if counts[i] < reach]
        whole, left = sum([portions[i] for i in movable]), spare
        for i in movable:
            addition = min(reach - counts[i], max(1, left * portions[i] // whole), spare)
            counts[i] = counts[i] + addition
            spare = spare - addition
    return np.array([reach] + counts)


def uneven(rng, amount, total, bound, skew):
    if amount == 2:
        one = jax.random.randint(rng, (), max(1, total - bound), min(bound, total - 1) + 1)
        return jnp.stack([one, total - one])
    sizes = jnp.asarray(split_up(amount, total, bound, skew), jnp.int32)
    pairs = (amount - 1) // 2
    giver, taker = sizes[1:1 + 2 * pairs:2], sizes[2:2 + 2 * pairs:2]
    room = jnp.minimum(giver - 1, bound - taker)
    passed = jax.random.randint(jax.random.fold_in(rng, 1), (pairs,), 0, 1 << 20) % (room + 1)
    sizes = sizes.at[1:1 + 2 * pairs:2].set(giver - passed).at[2:2 + 2 * pairs:2].set(taker + passed)
    return sizes[jax.random.permutation(jax.random.fold_in(rng, 2), amount)]


def scatter_about(rng, dims, scale, reach, shards=(), held_as=jnp.bfloat16):
    drawn = scale * jax.random.normal(rng, dims, jnp.float32)
    if shards:
        drawn = drawn * shard_levels(rng, dims, shards, -0.22, 0.18)
    return jnp.clip(drawn, -reach, reach).astype(held_as)


def setup_inputs(seed: int = 0) -> dict:
    arg_keys = jax.random.split(jax.random.key(seed), 6)
    return {
        "queries": draw_queries(jax.random.fold_in(arg_keys[5], 71), 0),
        "key_states": draw_key_states(jax.random.fold_in(arg_keys[5], 71), 0),
        "value_states": scatter_about(arg_keys[2], (TOKENS, KV_HEADS * HEAD), 1.0, 6.0, ((0, 32),)),
        "grad_out": scatter_about(arg_keys[3], (TOKENS, HEADS * HEAD), 1.0, 6.0, ((0, 32),)),
        "doc_ids": jnp.searchsorted(jnp.cumsum(uneven(arg_keys[4], NDOCS, TOKENS, MAXDOC, 0)), jnp.arange(TOKENS), side="right").astype(jnp.int32),
    }


def attend(query_head, key_head, value_head, grad_head, allowed):
    softmax_scale = HEAD ** -0.5
    query_full = query_head.astype(jnp.float32)
    key_full = key_head.astype(jnp.float32)
    value_full = value_head.astype(jnp.float32)
    grad_full = grad_head.astype(jnp.float32)
    scores = jnp.einsum("igd,jd->gij", query_full, key_full) * softmax_scale
    scores = jnp.where(allowed[None], scores, -jnp.inf)
    row_max = jnp.max(scores, axis=-1, keepdims=True)
    log_total = row_max + jnp.log(jnp.sum(jnp.exp(scores - row_max), axis=-1, keepdims=True))
    weights = jnp.where(allowed[None], jnp.exp(scores - log_total), 0.0)
    probs_low = weights.astype(jnp.bfloat16)
    output = jnp.einsum("gij,jd->igd", probs_low.astype(jnp.float32), value_full).astype(jnp.bfloat16)
    row_delta = jnp.sum(grad_full * output.astype(jnp.float32), axis=-1)
    grad_probs = jnp.einsum("igd,jd->gij", grad_full, value_full)
    grad_scores = (weights * (grad_probs - row_delta.T[:, :, None]) * softmax_scale).astype(jnp.bfloat16)
    grad_scores_full = grad_scores.astype(jnp.float32)
    grad_query = jnp.einsum("gij,jd->igd", grad_scores_full, key_full).astype(jnp.bfloat16)
    grad_key = jnp.einsum("gij,igd->jd", grad_scores_full, query_full)
    grad_value = jnp.einsum("gij,igd->jd", probs_low.astype(jnp.float32), grad_full)
    return output, grad_query, grad_key, grad_value


def reference(queries, key_states, value_states, grad_out, doc_ids):
    blocks = TOKENS // TOK_DEV
    margin = (WINDOW - 1) * TOK_DEV
    window_len = WINDOW * TOK_DEV
    groups = HEADS // KV_HEADS
    key_padded = jnp.concatenate([jnp.zeros((margin, KV_HEADS * HEAD), key_states.dtype), key_states], 0)
    value_padded = jnp.concatenate([jnp.zeros((margin, KV_HEADS * HEAD), value_states.dtype), value_states], 0)
    ids_padded = jnp.concatenate([jnp.full((margin,), -1, jnp.int32), doc_ids.astype(jnp.int32)], 0)
    query_index = jnp.arange(TOK_DEV, dtype=jnp.int32)
    window_index = jnp.arange(window_len, dtype=jnp.int32)
    vmapped = jax.vmap(attend, in_axes=(1, 1, 1, 1, None), out_axes=(1, 1, 1, 1))

    def one_block(totals, block_id):
        grad_keys, grad_values = totals
        first_row = (block_id * TOK_DEV).astype(jnp.int32)
        query_rows = lax.dynamic_slice_in_dim(queries, first_row, TOK_DEV, 0).reshape(TOK_DEV, KV_HEADS, groups, HEAD)
        grad_rows = lax.dynamic_slice_in_dim(grad_out, first_row, TOK_DEV, 0).reshape(TOK_DEV, KV_HEADS, groups, HEAD)
        query_ids = lax.dynamic_slice_in_dim(doc_ids.astype(jnp.int32), first_row, TOK_DEV, 0)
        key_rows = lax.dynamic_slice_in_dim(key_padded, first_row, window_len, 0).reshape(window_len, KV_HEADS, HEAD)
        value_rows = lax.dynamic_slice_in_dim(value_padded, first_row, window_len, 0).reshape(window_len, KV_HEADS, HEAD)
        key_ids = lax.dynamic_slice_in_dim(ids_padded, first_row, window_len, 0)
        allowed = (key_ids[None, :] == query_ids[:, None]) & (window_index[None, :] - margin <= query_index[:, None])
        output, grad_query, grad_key, grad_value = vmapped(query_rows, key_rows, value_rows, grad_rows, allowed)
        old_keys = lax.dynamic_slice_in_dim(grad_keys, first_row, window_len, 0)
        grad_keys = lax.dynamic_update_slice_in_dim(grad_keys, old_keys + grad_key.reshape(window_len, KV_HEADS * HEAD), first_row, 0)
        old_values = lax.dynamic_slice_in_dim(grad_values, first_row, window_len, 0)
        grad_values = lax.dynamic_update_slice_in_dim(grad_values, old_values + grad_value.reshape(window_len, KV_HEADS * HEAD), first_row, 0)
        return (grad_keys, grad_values), (output.reshape(TOK_DEV, HEADS * HEAD), grad_query.reshape(TOK_DEV, HEADS * HEAD))

    zero_field = jnp.zeros((TOKENS + margin, KV_HEADS * HEAD), jnp.float32)
    (grad_keys, grad_values), (outputs, grad_queries) = lax.scan(one_block, (zero_field, zero_field), jnp.arange(blocks, dtype=jnp.int32))
    return (outputs.reshape(TOKENS, HEADS * HEAD), grad_queries.reshape(TOKENS, HEADS * HEAD), grad_keys[margin:].astype(jnp.bfloat16), grad_values[margin:].astype(jnp.bfloat16))
```

```python
import functools

import jax
import jax.numpy as jnp
from jax import lax
from jax.experimental import pallas as pl
from jax.experimental.pallas import tpu as pltpu
from jax.sharding import PartitionSpec as P

HEADS = 16
KV_HEADS = 4
HEAD = 128
WINDOW = 8
AXES = ("dp", "group")
GROUPS = HEADS // KV_HEADS
EXTRA = 16
PAIR = 2

VMEM = pl.BlockSpec(memory_space=pltpu.VMEM)
SMEM = pl.BlockSpec(memory_space=pltpu.SMEM)
BF16 = jnp.bfloat16
F32 = jnp.float32


def rows_at(index, rows):
    return pl.ds(pl.multiple_of(index * rows, rows), rows)


def call(kernel, name, outs, operands, scratch=()):
    return pl.pallas_call(
        kernel,
        out_shape=[jax.ShapeDtypeStruct(shape, dtype) for shape, dtype in outs],
        in_specs=[SMEM] + [VMEM] * (len(operands) - 1),
        out_specs=[VMEM] * len(outs),
        scratch_shapes=list(scratch),
        compiler_params=pltpu.CompilerParams(vmem_limit_bytes=48 * 1024 * 1024),
        name=name,
    )(*operands)


def pack_keys(tok, info, ids, keys, values, *slots):
    me = info[0]
    along = jnp.broadcast_to(ids[...], (tok, tok)).astype(F32)
    down = along.T
    local_start = jnp.sum((down < along).astype(F32), axis=0, keepdims=True)
    low = (ids[...] & 255).astype(F32)
    high = (ids[...] >> 8).astype(F32)
    marks = jnp.concatenate(
        [local_start, low, high, jnp.zeros((EXTRA - 3, tok), F32)], 0
    ).astype(BF16)
    for s, slot in enumerate(slots):
        columns = rows_at(me ^ s, HEAD)
        slot[0:tok, :] = keys[:, columns]
        slot[tok : 2 * tok, :] = values[:, columns]
        slot[2 * tok : 2 * tok + EXTRA, :] = marks


def pack_queries(tok, info, queries, grads, *slots):
    me = info[0]
    for s, slot in enumerate(slots):
        columns = rows_at(me ^ s, GROUPS * HEAD)
        slot[0:tok, :] = queries[:, columns]
        slot[tok : 2 * tok, :] = grads[:, columns]


def order_keys(tok, info, s0, s1, s2, s3, near, far):
    me = info[0]
    n = KV_HEADS
    for s, slot in enumerate((s0, s1, s2, s3)):
        block = me ^ s
        near[rows_at(block, tok), :] = slot[0:tok, :]
        near[rows_at(n + block, tok), :] = slot[tok : 2 * tok, :]
        near[pl.ds(pl.multiple_of(2 * n * tok + block * EXTRA, EXTRA), EXTRA), :] = slot[
            2 * tok : 2 * tok + EXTRA, :
        ]
    far[0 : 3 * tok, :] = near[tok : n * tok, :]
    far[3 * tok : 6 * tok, :] = near[(n + 1) * tok : 2 * n * tok, :]
    far[6 * tok :, :] = near[2 * n * tok + EXTRA :, :]


def attend(
    tok, info, own, near, far, q0, q1, q2, q3,
    r0, r1, r2, r3, own_terms, near_terms, far_terms,
    key_rows, value_rows, key_cols, value_cols, query_rows, grad_rows, marks, grad_keys, grad_values,
):
    me, quad = info[0], info[1]
    n = KV_HEADS
    span = WINDOW * tok
    before = span - tok
    blocks = 3 * n - 1
    key_rows[0 : 3 * tok, :] = far[0 : 3 * tok, :]
    key_rows[3 * tok : 7 * tok, :] = near[0 : 4 * tok, :]
    key_rows[7 * tok :, :] = own[0 : 4 * tok, :]
    value_rows[0 : 3 * tok, :] = far[3 * tok : 6 * tok, :]
    value_rows[3 * tok : 7 * tok, :] = near[4 * tok : 8 * tok, :]
    value_rows[7 * tok :, :] = own[4 * tok : 8 * tok, :]
    for b in range(blocks):
        at = slice(b * tok, (b + 1) * tok)
        key_cols[:, at] = key_rows[at, :].T
        value_cols[:, at] = value_rows[at, :].T
        if b < 3:
            mark = far[6 * tok + b * EXTRA : 6 * tok + (b + 1) * EXTRA, :]
        elif b < 7:
            mark = near[8 * tok + (b - 3) * EXTRA : 8 * tok + (b - 2) * EXTRA, :]
        else:
            mark = own[8 * tok + (b - 7) * EXTRA : 8 * tok + (b - 6) * EXTRA, :]
        mark = mark.astype(F32)
        ids = mark[1:2] + 256.0 * mark[2:3]
        exists = (quad - 2) * n + b + 1 >= 0
        marks[b : b + 1, :] = jnp.where(exists, ids, -1.0)
        if b >= 7:
            marks[16 + b - 7 : 17 + b - 7, :] = mark[0:1]
    for b in range(blocks, 16):
        marks[b : b + 1, :] = jnp.full((1, tok), -1.0, F32)
    for s, slot in enumerate((q0, q1, q2, q3)):
        for h in range(GROUPS):
            at = slice(h * tok, (h + 1) * tok)
            query_rows[s, at, :] = slot[0:tok, h * HEAD : (h + 1) * HEAD]
            grad_rows[s, at, :] = slot[tok : 2 * tok, h * HEAD : (h + 1) * HEAD]
    grad_keys[...] = jnp.zeros_like(grad_keys)
    grad_values[...] = jnp.zeros_like(grad_values)
    scale = HEAD ** (-0.5)
    key_place = lax.broadcasted_iota(jnp.int32, (span, tok), 0)
    query_limit = before + lax.broadcasted_iota(jnp.int32, (1, tok), 1)
    mark_row = lax.broadcasted_iota(jnp.int32, (16, tok), 0)

    for s, result in enumerate((r0, r1, r2, r3)):
        block = me ^ s
        window = rows_at(block, tok)
        window = pl.ds(pl.multiple_of(block * tok, tok), span)
        all_ids = marks[0:16, :]
        first = jnp.min(marks[pl.ds(block + 7, 1), :], axis=1, keepdims=True)
        earlier = (mark_row >= block) & (mark_row < block + 7) & (all_ids < first)
        count = jnp.sum(
            jnp.sum(earlier.astype(F32), axis=1, keepdims=True), axis=0, keepdims=True
        )
        local_start = marks[pl.ds(16 + block, 1), :]
        start = jnp.where(local_start == 0.0, count, before + local_start).astype(jnp.int32)
        allowed = (key_place >= start) & (key_place <= query_limit)
        bias = jnp.where(allowed, 0.0, -jnp.inf)
        bias = jnp.concatenate([bias] * PAIR, 1)

        def heads(i, carry):
            at = pl.ds(pl.multiple_of(i * PAIR * tok, PAIR * tok), PAIR * tok)
            query, grad = query_rows[s, at, :], grad_rows[s, at, :]
            scores = lax.dot_general(
                key_rows[window, :], query, (((1,), (1,)), ((), ())), preferred_element_type=F32
            )
            scores = scores + bias
            top = jnp.max(scores, axis=0, keepdims=True)
            weights = jnp.exp((scores - top) * scale)
            total = jnp.sum(weights, axis=0, keepdims=True)
            probs = weights * (1.0 / total)
            probs_low = probs.astype(BF16)
            output = jnp.dot(value_cols[:, window], probs_low, preferred_element_type=F32)
            output = output.astype(BF16).astype(F32)
            grad_probs = lax.dot_general(
                value_rows[window, :], grad, (((1,), (1,)), ((), ())), preferred_element_type=F32
            )
            grad_cols = jnp.concatenate(
                [grad[h * tok : (h + 1) * tok].T for h in range(PAIR)], 1
            ).astype(F32)
            delta = jnp.sum(grad_cols * output, axis=0, keepdims=True)
            grad_scores = (probs * (grad_probs - delta)).astype(BF16)
            grad_query = jnp.dot(key_cols[:, window], grad_scores, preferred_element_type=F32)
            grad_query = grad_query * scale
            grad_values[window, :] += jnp.dot(probs_low, grad, preferred_element_type=F32)
            grad_keys[window, :] += jnp.dot(grad_scores, query, preferred_element_type=F32)
            for h in range(PAIR):
                part = slice(h * tok, (h + 1) * tok)
                columns = pl.ds(pl.multiple_of((i * PAIR + h) * HEAD, HEAD), HEAD)
                result[0:tok, columns] = output[:, part].T.astype(BF16)
                result[tok : 2 * tok, columns] = grad_query[:, part].T.astype(BF16)
            return carry

        lax.fori_loop(0, GROUPS // PAIR, heads, 0)

    far_terms[0 : 3 * tok, :] = (grad_keys[0 : 3 * tok, :] * scale).astype(BF16)
    far_terms[3 * tok :, :] = grad_values[0 : 3 * tok, :].astype(BF16)
    near_terms[0 : 4 * tok, :] = (grad_keys[3 * tok : 7 * tok, :] * scale).astype(BF16)
    near_terms[4 * tok :, :] = grad_values[3 * tok : 7 * tok, :].astype(BF16)
    own_terms[0 : 4 * tok, :] = grad_keys[7 * tok :, :] * scale
    own_terms[4 * tok :, :] = grad_values[7 * tok :, :]


def add_terms(tok, info, own, near, far, s0, s1, s2, s3, total):
    me = info[0]
    n = KV_HEADS
    total[...] = own[...] + near[...].astype(F32)
    total[tok : n * tok, :] += far[0 : 3 * tok, :].astype(F32)
    total[(n + 1) * tok :, :] += far[3 * tok :, :].astype(F32)
    for s, slot in enumerate((s0, s1, s2, s3)):
        slot[0:tok, :] = total[rows_at(me ^ s, tok), :].astype(BF16)
        slot[tok : 2 * tok, :] = total[rows_at(n + (me ^ s), tok), :].astype(BF16)


def place_columns(tok, width, info, s0, s1, s2, s3, upper, lower):
    me = info[0]
    for s, slot in enumerate((s0, s1, s2, s3)):
        columns = rows_at(me ^ s, width)
        upper[:, columns] = slot[0:tok, :]
        lower[:, columns] = slot[tok : 2 * tok, :]


def local(queries, key_states, value_states, grad_out, doc_ids):
    tok = queries.shape[0]
    n = KV_HEADS
    count = lax.axis_size("dp") * lax.axis_size("group")
    rank = lax.axis_index(AXES)
    info = jnp.stack([rank % n, rank // n]).astype(jnp.int32)

    def swap(value, bits):
        return lax.ppermute(value, AXES, [(i, i ^ bits) for i in range(count)])

    def ring(value, steps):
        return lax.ppermute(value, AXES, [(i, (i + steps) % count) for i in range(count)])

    def exchange(slots):
        return [slots[0]] + [swap(slots[s], s) for s in range(1, n)]

    kv_slots = call(
        functools.partial(pack_keys, tok),
        "pack_keys",
        [((2 * tok + EXTRA, HEAD), BF16)] * n,
        (info, doc_ids[None, :], key_states, value_states),
    )
    kv_slots = exchange(kv_slots)
    query_slots = call(
        functools.partial(pack_queries, tok),
        "pack_queries",
        [((2 * tok, GROUPS * HEAD), BF16)] * n,
        (info, queries, grad_out),
    )
    query_slots = exchange(query_slots)
    own, own_late = call(
        functools.partial(order_keys, tok),
        "order_keys",
        [((2 * n * tok + n * EXTRA, HEAD), BF16), ((6 * tok + 3 * EXTRA, HEAD), BF16)],
        (info, *kv_slots),
    )
    near = ring(own, n)
    far = ring(own_late, 2 * n)
    blocks = 3 * n - 1
    results = call(
        functools.partial(attend, tok),
        "attend",
        [((2 * tok, GROUPS * HEAD), BF16)] * n
        + [((2 * n * tok, HEAD), F32), ((2 * n * tok, HEAD), BF16), ((6 * tok, HEAD), BF16)],
        (info, own, near, far, *query_slots),
        [
            pltpu.VMEM((blocks * tok, HEAD), BF16),
            pltpu.VMEM((blocks * tok, HEAD), BF16),
            pltpu.VMEM((HEAD, blocks * tok), BF16),
            pltpu.VMEM((HEAD, blocks * tok), BF16),
            pltpu.VMEM((n, GROUPS * tok, HEAD), BF16),
            pltpu.VMEM((n, GROUPS * tok, HEAD), BF16),
            pltpu.VMEM((24, tok), F32),
            pltpu.VMEM((blocks * tok, HEAD), F32),
            pltpu.VMEM((blocks * tok, HEAD), F32),
        ],
    )
    out_slots, (own_terms, near_terms, far_terms) = results[:n], results[n:]
    near_back = ring(near_terms, -n)
    far_back = ring(far_terms, -2 * n)
    out_slots = exchange(out_slots)
    grad_slots = call(
        functools.partial(add_terms, tok),
        "add_terms",
        [((2 * tok, HEAD), BF16)] * n,
        (info, own_terms, near_back, far_back),
        [pltpu.VMEM((2 * n * tok, HEAD), F32)],
    )
    grad_slots = exchange(grad_slots)
    attended, grad_queries = call(
        functools.partial(place_columns, tok, GROUPS * HEAD),
        "place_queries",
        [((tok, HEADS * HEAD), BF16)] * 2,
        (info, *out_slots),
    )
    grad_keys, grad_values = call(
        functools.partial(place_columns, tok, HEAD),
        "place_keys",
        [((tok, KV_HEADS * HEAD), BF16)] * 2,
        (info, *grad_slots),
    )
    return (attended, grad_queries, grad_keys, grad_values)


def solution(mesh):
    rows = P(AXES, None)
    return jax.shard_map(
        local,
        mesh=mesh,
        in_specs=(rows, rows, rows, rows, P(AXES)),
        out_specs=(rows, rows, rows, rows),
        check_vma=False,
    )
```

```python
import functools
import math

import jax
import jax.numpy as jnp
from jax import lax
from jax.experimental import pallas as pl
from jax.experimental.pallas import tpu as pltpu
from jax.sharding import PartitionSpec as P

HEADS = 16
KV_HEADS = 4
HEAD = 128
WINDOW = 8
AXES = ("dp", "group")
GROUPS = HEADS // KV_HEADS
EXTRA = 16

VMEM = pl.BlockSpec(memory_space=pltpu.VMEM)
SMEM = pl.BlockSpec(memory_space=pltpu.SMEM)
ANY = pl.BlockSpec(memory_space=pl.ANY)
BF16 = jnp.bfloat16
F32 = jnp.float32


def rows_at(index, rows):
    return pl.ds(pl.multiple_of(index * rows, rows), rows)


def call(kernel, name, outs, operands, scratch=(), in_space=VMEM, out_space=VMEM):
    return pl.pallas_call(
        kernel,
        out_shape=[jax.ShapeDtypeStruct(shape, dtype) for shape, dtype in outs],
        in_specs=[SMEM] + [in_space] * (len(operands) - 1),
        out_specs=[out_space] * len(outs),
        scratch_shapes=list(scratch),
        compiler_params=pltpu.CompilerParams(vmem_limit_bytes=48 * 1024 * 1024),
        name=name,
    )(*operands)


def in_hbm(value):
    return pltpu.with_memory_space_constraint(value, pltpu.HBM)


def copy_all(pairs, sems):
    copies = [pltpu.make_async_copy(a, b, sems.at[i]) for i, (a, b) in enumerate(pairs)]
    for copy in copies:
        copy.start()
    return copies


def wait_all(copies):
    for copy in copies:
        copy.wait()


def pack_keys(tok, info, ids, keys, values, s0, s1, s2, s3, ids_here, sems):
    me = info[0]
    slots = (s0, s1, s2, s3)
    pairs = [(ids, ids_here)]
    for s, slot in enumerate(slots):
        columns = rows_at(me ^ s, HEAD)
        pairs.append((keys.at[:, columns], slot.at[0:tok, :]))
        pairs.append((values.at[:, columns], slot.at[tok : 2 * tok, :]))
    copies = copy_all(pairs, sems)
    copies[0].wait()
    along = jnp.broadcast_to(ids_here[...], (tok, tok)).astype(F32)
    down = along.T
    local_start = jnp.sum((down < along).astype(F32), axis=0, keepdims=True)
    low = (ids_here[...] & 255).astype(F32)
    high = (ids_here[...] >> 8).astype(F32)
    marks = jnp.concatenate(
        [local_start, low, high, jnp.zeros((EXTRA - 3, tok), F32)], 0
    ).astype(BF16)
    for slot in slots:
        slot[2 * tok : 2 * tok + EXTRA, :] = marks
    wait_all(copies[1:])


def pack_queries(tok, info, queries, grads, s0, s1, s2, s3, sems):
    me = info[0]
    pairs = []
    for s, slot in enumerate((s0, s1, s2, s3)):
        columns = rows_at(me ^ s, GROUPS * HEAD)
        pairs.append((queries.at[:, columns], slot.at[0:tok, :]))
        pairs.append((grads.at[:, columns], slot.at[tok : 2 * tok, :]))
    copies = copy_all(pairs, sems)
    for slot in (s1, s2, s3):
        slot[2 * tok :, :] = jnp.zeros((slot.shape[0] - 2 * tok, slot.shape[1]), BF16)
    wait_all(copies)


def order_keys(tok, info, s0, s1, s2, s3, near, far, marks):
    me = info[0]
    n = KV_HEADS
    marks[...] = jnp.zeros_like(marks)
    for s, slot in enumerate((s0, s1, s2, s3)):
        block = me ^ s
        near[rows_at(block, tok), :] = slot[0:tok, :]
        near[rows_at(n + block, tok), :] = slot[tok : 2 * tok, :]
        mark = slot[2 * tok : 2 * tok + EXTRA, :].astype(F32)
        for kind in range(3):
            marks[pl.ds(kind * n + block, 1), :] = mark[kind : kind + 1]
    near[2 * n * tok :, :] = marks[...].astype(BF16)
    far[0 : 3 * tok, :] = near[tok : n * tok, :]
    far[3 * tok : 6 * tok, :] = near[(n + 1) * tok : 2 * n * tok, :]
    far[6 * tok :, :] = near[2 * n * tok :, :]


def attend(
    tok, info, own, near, far, q0, q1, q2, q3,
    r0, r1, r2, r3, own_terms, near_terms, far_terms,
    key_rows, value_rows, key_cols, value_cols, marks, grad_keys, grad_values,
):
    me, quad = info[0], info[1]
    n = KV_HEADS
    span = WINDOW * tok
    before = span - tok
    blocks = 3 * n - 1
    key_rows[0 : 3 * tok, :] = far[0 : 3 * tok, :]
    key_rows[3 * tok : 7 * tok, :] = near[0 : 4 * tok, :]
    key_rows[7 * tok :, :] = own[0 : 4 * tok, :]
    value_rows[0 : 3 * tok, :] = far[3 * tok : 6 * tok, :]
    value_rows[3 * tok : 7 * tok, :] = near[4 * tok : 8 * tok, :]
    value_rows[7 * tok :, :] = own[4 * tok : 8 * tok, :]
    for b in range(blocks):
        at = slice(b * tok, (b + 1) * tok)
        key_cols[:, at] = key_rows[at, :].T
        value_cols[:, at] = value_rows[at, :].T
    for first, count, source in ((0, 3, far), (3, 4, near), (7, 4, own)):
        mark = source[source.shape[0] - EXTRA :, :].astype(F32)
        ids = mark[n : 2 * n] + 256.0 * mark[2 * n : 3 * n]
        exists = (quad - 2) * n + first + 1 >= 0
        marks[first : first + count, :] = jnp.where(exists, ids[n - count : n], -1.0)
        if source is own:
            marks[16 : 16 + n, :] = mark[0:n]
    marks[blocks:16, :] = jnp.full((16 - blocks, tok), -1.0, F32)
    grad_keys[...] = jnp.zeros_like(grad_keys)
    grad_values[...] = jnp.zeros_like(grad_values)
    scale = HEAD ** (-0.5)
    key_place = lax.broadcasted_iota(jnp.int32, (span, tok), 0)
    query_limit = before + lax.broadcasted_iota(jnp.int32, (1, tok), 1)
    mark_row = lax.broadcasted_iota(jnp.int32, (16, tok), 0)

    for s, (piece, result) in enumerate(((q0, r0), (q1, r1), (q2, r2), (q3, r3))):
        block = me ^ s
        window = pl.ds(pl.multiple_of(block * tok, tok), span)
        all_ids = marks[0:16, :]
        first = jnp.min(marks[pl.ds(block + 7, 1), :], axis=1, keepdims=True)
        earlier = (mark_row >= block) & (mark_row < block + 7) & (all_ids < first)
        count = jnp.sum(
            jnp.sum(earlier.astype(F32), axis=1, keepdims=True), axis=0, keepdims=True
        )
        local_start = marks[pl.ds(16 + block, 1), :]
        start = jnp.where(local_start == 0.0, count, before + local_start).astype(jnp.int32)
        allowed = (key_place >= start) & (key_place <= query_limit)
        bias = jnp.where(allowed, 0.0, -jnp.inf)
        bias = jnp.concatenate([bias] * GROUPS, 1)
        query = jnp.concatenate(
            [piece[0:tok, h * HEAD : (h + 1) * HEAD] for h in range(GROUPS)], 0
        )
        grad = jnp.concatenate(
            [piece[tok : 2 * tok, h * HEAD : (h + 1) * HEAD] for h in range(GROUPS)], 0
        )
        scores = lax.dot_general(
            key_rows[window, :], query, (((1,), (1,)), ((), ())), preferred_element_type=F32
        )
        scores = scores + bias
        top = jnp.max(scores, axis=0, keepdims=True)
        weights = jnp.exp2((scores - top) * (scale * math.log2(math.e)))
        total = jnp.sum(weights, axis=0, keepdims=True)
        probs = weights * (1.0 / total)
        probs_low = probs.astype(BF16)
        output = jnp.dot(value_cols[:, window], probs_low, preferred_element_type=F32)
        output = output.astype(BF16).astype(F32)
        grad_probs = lax.dot_general(
            value_rows[window, :], grad, (((1,), (1,)), ((), ())), preferred_element_type=F32
        )
        grad_cols = jnp.concatenate(
            [grad[h * tok : (h + 1) * tok].T for h in range(GROUPS)], 1
        ).astype(F32)
        delta = jnp.sum(grad_cols * output, axis=0, keepdims=True)
        grad_scores = (probs * (grad_probs - delta)).astype(BF16)
        grad_query = jnp.dot(key_cols[:, window], grad_scores, preferred_element_type=F32)
        grad_query = grad_query * scale
        grad_values[window, :] += jnp.dot(probs_low, grad, preferred_element_type=F32)
        grad_keys[window, :] += jnp.dot(grad_scores, query, preferred_element_type=F32)
        for h in range(GROUPS):
            part = slice(h * tok, (h + 1) * tok)
            columns = slice(h * HEAD, (h + 1) * HEAD)
            result[0:tok, columns] = output[:, part].T.astype(BF16)
            result[tok : 2 * tok, columns] = grad_query[:, part].T.astype(BF16)

    far_terms[0 : 3 * tok, :] = (grad_keys[0 : 3 * tok, :] * scale).astype(BF16)
    far_terms[3 * tok :, :] = grad_values[0 : 3 * tok, :].astype(BF16)
    near_terms[0 : 4 * tok, :] = (grad_keys[3 * tok : 7 * tok, :] * scale).astype(BF16)
    near_terms[4 * tok :, :] = grad_values[3 * tok : 7 * tok, :].astype(BF16)
    own_terms[0 : 4 * tok, :] = grad_keys[7 * tok :, :] * scale
    own_terms[4 * tok :, :] = grad_values[7 * tok :, :]


def add_terms(tok, info, own, near, far, s0, s1, s2, s3, total):
    me = info[0]
    n = KV_HEADS
    total[...] = own[...] + near[...].astype(F32)
    total[tok : n * tok, :] += far[0 : 3 * tok, :].astype(F32)
    total[(n + 1) * tok :, :] += far[3 * tok :, :].astype(F32)
    for s, slot in enumerate((s0, s1, s2, s3)):
        slot[0:tok, :] = total[rows_at(me ^ s, tok), :].astype(BF16)
        slot[tok : 2 * tok, :] = total[rows_at(n + (me ^ s), tok), :].astype(BF16)


def place_columns(tok, width, info, s0, s1, s2, s3, upper, lower, sems):
    me = info[0]
    pairs = []
    for s, slot in enumerate((s0, s1, s2, s3)):
        columns = rows_at(me ^ s, width)
        pairs.append((slot.at[0:tok], upper.at[:, columns]))
        pairs.append((slot.at[tok : 2 * tok], lower.at[:, columns]))
    wait_all(copy_all(pairs, sems))


def local(queries, key_states, value_states, grad_out, doc_ids):
    tok = queries.shape[0]
    n = KV_HEADS
    count = lax.axis_size("dp") * lax.axis_size("group")
    rank = lax.axis_index(AXES)
    info = jnp.stack([rank % n, rank // n]).astype(jnp.int32)

    def swap(value, bits):
        return lax.ppermute(value, AXES, [(i, i ^ bits) for i in range(count)])

    def ring(value, steps):
        return lax.ppermute(value, AXES, [(i, (i + steps) % count) for i in range(count)])

    def exchange(slots):
        return [slots[0]] + [swap(slots[s], s) for s in range(1, n)]

    dma = pltpu.SemaphoreType.DMA
    kv_slots = call(
        functools.partial(pack_keys, tok),
        "pack_keys",
        [((2 * tok + EXTRA, HEAD), BF16)] * n,
        (info, in_hbm(doc_ids[None, :]), in_hbm(key_states), in_hbm(value_states)),
        [pltpu.VMEM((1, tok), jnp.int32), dma((9,))],
        in_space=ANY,
    )
    kv_slots = exchange(kv_slots)
    query_slots = call(
        functools.partial(pack_queries, tok),
        "pack_queries",
        [((2 * tok + EXTRA, GROUPS * HEAD), BF16)] * n,
        (info, in_hbm(queries), in_hbm(grad_out)),
        [dma((8,))],
        in_space=ANY,
    )
    query_slots = exchange(query_slots)
    own, own_late = call(
        functools.partial(order_keys, tok),
        "order_keys",
        [((2 * n * tok + EXTRA, HEAD), BF16), ((6 * tok + EXTRA, HEAD), BF16)],
        (info, *kv_slots),
        [pltpu.VMEM((EXTRA, HEAD), F32)],
    )
    near = ring(own, n)
    far = ring(own_late, 2 * n)
    blocks = 3 * n - 1
    results = call(
        functools.partial(attend, tok),
        "attend",
        [((2 * tok, GROUPS * HEAD), BF16)] * n
        + [((2 * n * tok, HEAD), F32), ((2 * n * tok, HEAD), BF16), ((6 * tok, HEAD), BF16)],
        (info, own, near, far, *query_slots),
        [
            pltpu.VMEM((blocks * tok, HEAD), BF16),
            pltpu.VMEM((blocks * tok, HEAD), BF16),
            pltpu.VMEM((HEAD, blocks * tok), BF16),
            pltpu.VMEM((HEAD, blocks * tok), BF16),
            pltpu.VMEM((24, tok), F32),
            pltpu.VMEM((blocks * tok, HEAD), F32),
            pltpu.VMEM((blocks * tok, HEAD), F32),
        ],
    )
    out_slots, (own_terms, near_terms, far_terms) = results[:n], results[n:]
    near_back = ring(near_terms, -n)
    far_back = ring(far_terms, -2 * n)
    out_slots = exchange(out_slots)
    grad_slots = call(
        functools.partial(add_terms, tok),
        "add_terms",
        [((2 * tok, HEAD), BF16)] * n,
        (info, own_terms, near_back, far_back),
        [pltpu.VMEM((2 * n * tok, HEAD), F32)],
    )
    grad_slots = exchange(grad_slots)
    attended, grad_queries = call(
        functools.partial(place_columns, tok, GROUPS * HEAD),
        "place_queries",
        [((tok, HEADS * HEAD), BF16)] * 2,
        (info, *out_slots),
        [dma((8,))],
        out_space=ANY,
    )
    grad_keys, grad_values = call(
        functools.partial(place_columns, tok, HEAD),
        "place_keys",
        [((tok, KV_HEADS * HEAD), BF16)] * 2,
        (info, *grad_slots),
        [dma((8,))],
        out_space=ANY,
    )
    return (attended, grad_queries, grad_keys, grad_values)


def solution(mesh):
    rows = P(AXES, None)
    return jax.shard_map(
        local,
        mesh=mesh,
        in_specs=(rows, rows, rows, rows, P(AXES)),
        out_specs=(rows, rows, rows, rows),
        check_vma=False,
    )
```

```python
import functools
import math

import jax
import jax.numpy as jnp
from jax import lax
from jax.experimental import pallas as pl
from jax.experimental.pallas import tpu as pltpu
from jax.sharding import PartitionSpec as P

HEADS = 16
KV_HEADS = 4
HEAD = 128
WINDOW = 8
AXES = ("dp", "group")
GROUPS = HEADS // KV_HEADS
EXTRA = 16
SKIPS = (0, 2, 4)

VMEM = pl.BlockSpec(memory_space=pltpu.VMEM)
SMEM = pl.BlockSpec(memory_space=pltpu.SMEM)
ANY = pl.BlockSpec(memory_space=pl.ANY)
BF16 = jnp.bfloat16
F32 = jnp.float32


def rows_at(index, rows):
    return pl.ds(pl.multiple_of(index * rows, rows), rows)


def call(kernel, name, outs, operands, scratch=(), in_space=VMEM, out_space=VMEM):
    return pl.pallas_call(
        kernel,
        out_shape=[jax.ShapeDtypeStruct(shape, dtype) for shape, dtype in outs],
        in_specs=[SMEM] + [in_space] * (len(operands) - 1),
        out_specs=[out_space] * len(outs),
        scratch_shapes=list(scratch),
        compiler_params=pltpu.CompilerParams(vmem_limit_bytes=48 * 1024 * 1024),
        name=name,
    )(*operands)


def in_hbm(value):
    return pltpu.with_memory_space_constraint(value, pltpu.HBM)


def copy_all(pairs, sems):
    copies = [pltpu.make_async_copy(a, b, sems.at[i]) for i, (a, b) in enumerate(pairs)]
    for copy in copies:
        copy.start()
    return copies


def wait_all(copies):
    for copy in copies:
        copy.wait()


def pack_keys(tok, info, ids, keys, values, s0, s1, s2, s3, ids_here, sems):
    me = info[0]
    slots = (s0, s1, s2, s3)
    pairs = [(ids, ids_here)]
    for s, slot in enumerate(slots):
        columns = rows_at(me ^ s, HEAD)
        pairs.append((keys.at[:, columns], slot.at[0:tok, :]))
        pairs.append((values.at[:, columns], slot.at[tok : 2 * tok, :]))
    copies = copy_all(pairs, sems)
    copies[0].wait()
    along = jnp.broadcast_to(ids_here[...], (tok, tok)).astype(F32)
    down = along.T
    local_start = jnp.sum((down < along).astype(F32), axis=0, keepdims=True)
    low = (ids_here[...] & 255).astype(F32)
    high = (ids_here[...] >> 8).astype(F32)
    marks = jnp.concatenate(
        [local_start, low, high, jnp.zeros((EXTRA - 3, tok), F32)], 0
    ).astype(BF16)
    for slot in slots:
        slot[2 * tok : 2 * tok + EXTRA, :] = marks
    wait_all(copies[1:])


def pack_queries(tok, info, queries, grads, s0, s1, s2, s3, sems):
    me = info[0]
    pairs = []
    for s, slot in enumerate((s0, s1, s2, s3)):
        columns = rows_at(me ^ s, GROUPS * HEAD)
        pairs.append((queries.at[:, columns], slot.at[0:tok, :]))
        pairs.append((grads.at[:, columns], slot.at[tok : 2 * tok, :]))
    copies = copy_all(pairs, sems)
    for slot in (s1, s2, s3):
        slot[2 * tok :, :] = jnp.zeros((slot.shape[0] - 2 * tok, slot.shape[1]), BF16)
    wait_all(copies)


def order_keys(tok, info, s0, s1, s2, s3, near, far, marks):
    me = info[0]
    n = KV_HEADS
    marks[...] = jnp.zeros_like(marks)
    for s, slot in enumerate((s0, s1, s2, s3)):
        block = me ^ s
        near[rows_at(block, tok), :] = slot[0:tok, :]
        near[rows_at(n + block, tok), :] = slot[tok : 2 * tok, :]
        mark = slot[2 * tok : 2 * tok + EXTRA, :].astype(F32)
        for kind in range(3):
            marks[pl.ds(kind * n + block, 1), :] = mark[kind : kind + 1]
    near[2 * n * tok :, :] = marks[...].astype(BF16)
    far[0 : 3 * tok, :] = near[tok : n * tok, :]
    far[3 * tok : 6 * tok, :] = near[(n + 1) * tok : 2 * n * tok, :]
    far[6 * tok :, :] = near[2 * n * tok :, :]


def attend(
    tok, info, own, near, far, q0, q1, q2, q3,
    r0, r1, r2, r3, own_terms, near_terms, far_terms,
    key_rows, value_rows, marks, grad_keys, grad_values,
):
    me, quad = info[0], info[1]
    n = KV_HEADS
    span = WINDOW * tok
    before = span - tok
    blocks = 3 * n - 1
    key_rows[0 : 3 * tok, :] = far[0 : 3 * tok, :]
    key_rows[3 * tok : 7 * tok, :] = near[0 : 4 * tok, :]
    key_rows[7 * tok :, :] = own[0 : 4 * tok, :]
    value_rows[0 : 3 * tok, :] = far[3 * tok : 6 * tok, :]
    value_rows[3 * tok : 7 * tok, :] = near[4 * tok : 8 * tok, :]
    value_rows[7 * tok :, :] = own[4 * tok : 8 * tok, :]
    for first, count, source in ((0, 3, far), (3, 4, near), (7, 4, own)):
        mark = source[source.shape[0] - EXTRA :, :].astype(F32)
        ids = mark[n : 2 * n] + 256.0 * mark[2 * n : 3 * n]
        exists = (quad - 2) * n + first + 1 >= 0
        marks[first : first + count, :] = jnp.where(exists, ids[n - count : n], -1.0)
        if source is own:
            marks[16 : 16 + n, :] = mark[0:n]
    marks[blocks:16, :] = jnp.full((16 - blocks, tok), -1.0, F32)
    grad_keys[...] = jnp.zeros_like(grad_keys)
    grad_values[...] = jnp.zeros_like(grad_values)
    scale = HEAD ** (-0.5)
    mark_row = lax.broadcasted_iota(jnp.int32, (16, tok), 0)

    def first_key(block):
        first = jnp.min(marks[pl.ds(block + 7, 1), :], axis=1, keepdims=True)
        earlier = (mark_row >= block) & (mark_row < block + 7) & (marks[0:16, :] < first)
        return jnp.sum(
            jnp.sum(earlier.astype(F32), axis=1, keepdims=True), axis=0, keepdims=True
        ).astype(jnp.int32)

    def attend_block(block, count, piece, result, skip):
        rows = span - skip * tok
        window = pl.ds(pl.multiple_of((block + skip) * tok, tok), rows)
        local_start = marks[pl.ds(16 + block, 1), :].astype(jnp.int32)
        start = jnp.where(local_start == 0, count, before + local_start) - skip * tok
        key_place = lax.broadcasted_iota(jnp.int32, (rows, tok), 0)
        query_limit = before - skip * tok + lax.broadcasted_iota(jnp.int32, (1, tok), 1)
        allowed = (key_place >= start) & (key_place <= query_limit)
        bias = jnp.where(allowed, 0.0, -jnp.inf)
        bias = jnp.concatenate([bias] * GROUPS, 1)
        query = jnp.concatenate(
            [piece[0:tok, h * HEAD : (h + 1) * HEAD] for h in range(GROUPS)], 0
        )
        grad = jnp.concatenate(
            [piece[tok : 2 * tok, h * HEAD : (h + 1) * HEAD] for h in range(GROUPS)], 0
        )
        scores = lax.dot_general(
            key_rows[window, :], query, (((1,), (1,)), ((), ())), preferred_element_type=F32
        )
        scores = scores + bias
        top = jnp.max(scores, axis=0, keepdims=True)
        weights = jnp.exp2((scores - top) * (scale * math.log2(math.e)))
        total = jnp.sum(weights, axis=0, keepdims=True)
        probs = weights * (1.0 / total)
        probs_low = probs.astype(BF16)
        output = lax.dot_general(
            value_rows[window, :], probs_low, (((0,), (0,)), ((), ())), preferred_element_type=F32
        )
        output = output.astype(BF16).astype(F32)
        grad_probs = lax.dot_general(
            value_rows[window, :], grad, (((1,), (1,)), ((), ())), preferred_element_type=F32
        )
        grad_cols = jnp.concatenate(
            [grad[h * tok : (h + 1) * tok].T for h in range(GROUPS)], 1
        ).astype(F32)
        delta = jnp.sum(grad_cols * output, axis=0, keepdims=True)
        grad_scores = (probs * (grad_probs - delta)).astype(BF16)
        grad_query = lax.dot_general(
            key_rows[window, :], grad_scores, (((0,), (0,)), ((), ())), preferred_element_type=F32
        )
        grad_query = grad_query * scale
        grad_values[window, :] += jnp.dot(probs_low, grad, preferred_element_type=F32)
        grad_keys[window, :] += jnp.dot(grad_scores, query, preferred_element_type=F32)
        for h in range(GROUPS):
            part = slice(h * tok, (h + 1) * tok)
            columns = slice(h * HEAD, (h + 1) * HEAD)
            result[0:tok, columns] = output[:, part].T.astype(BF16)
            result[tok : 2 * tok, columns] = grad_query[:, part].T.astype(BF16)

    counts = [first_key(me ^ s) for s in range(n)]
    whole = [count[0, 0] // tok for count in counts]
    for s, (piece, result) in enumerate(((q0, r0), (q1, r1), (q2, r2), (q3, r3))):
        for at, skip in enumerate(SKIPS):
            fits = whole[s] >= skip
            if at + 1 < len(SKIPS):
                fits = fits & (whole[s] < SKIPS[at + 1])
            pl.when(fits)(
                functools.partial(attend_block, me ^ s, counts[s], piece, result, skip)
            )

    far_terms[0 : 3 * tok, :] = (grad_keys[0 : 3 * tok, :] * scale).astype(BF16)
    far_terms[3 * tok :, :] = grad_values[0 : 3 * tok, :].astype(BF16)
    near_terms[0 : 4 * tok, :] = (grad_keys[3 * tok : 7 * tok, :] * scale).astype(BF16)
    near_terms[4 * tok :, :] = grad_values[3 * tok : 7 * tok, :].astype(BF16)
    own_terms[0 : 4 * tok, :] = grad_keys[7 * tok :, :] * scale
    own_terms[4 * tok :, :] = grad_values[7 * tok :, :]


def add_terms(tok, info, own, near, far, s0, s1, s2, s3, total):
    me = info[0]
    n = KV_HEADS
    total[...] = own[...] + near[...].astype(F32)
    total[tok : n * tok, :] += far[0 : 3 * tok, :].astype(F32)
    total[(n + 1) * tok :, :] += far[3 * tok :, :].astype(F32)
    for s, slot in enumerate((s0, s1, s2, s3)):
        slot[0:tok, :] = total[rows_at(me ^ s, tok), :].astype(BF16)
        slot[tok : 2 * tok, :] = total[rows_at(n + (me ^ s), tok), :].astype(BF16)


def place_columns(tok, width, info, s0, s1, s2, s3, upper, lower, sems):
    me = info[0]
    pairs = []
    for s, slot in enumerate((s0, s1, s2, s3)):
        columns = rows_at(me ^ s, width)
        pairs.append((slot.at[0:tok], upper.at[:, columns]))
        pairs.append((slot.at[tok : 2 * tok], lower.at[:, columns]))
    wait_all(copy_all(pairs, sems))


def local(queries, key_states, value_states, grad_out, doc_ids):
    tok = queries.shape[0]
    n = KV_HEADS
    count = lax.axis_size("dp") * lax.axis_size("group")
    rank = lax.axis_index(AXES)
    info = jnp.stack([rank % n, rank // n]).astype(jnp.int32)

    def swap(value, bits):
        return lax.ppermute(value, AXES, [(i, i ^ bits) for i in range(count)])

    def ring(value, steps):
        return lax.ppermute(value, AXES, [(i, (i + steps) % count) for i in range(count)])

    def exchange(slots):
        return [slots[0]] + [swap(slots[s], s) for s in range(1, n)]

    dma = pltpu.SemaphoreType.DMA
    kv_slots = call(
        functools.partial(pack_keys, tok),
        "pack_keys",
        [((2 * tok + EXTRA, HEAD), BF16)] * n,
        (info, in_hbm(doc_ids[None, :]), in_hbm(key_states), in_hbm(value_states)),
        [pltpu.VMEM((1, tok), jnp.int32), dma((9,))],
        in_space=ANY,
    )
    kv_slots = exchange(kv_slots)
    query_slots = call(
        functools.partial(pack_queries, tok),
        "pack_queries",
        [((2 * tok + EXTRA, GROUPS * HEAD), BF16)] * n,
        (info, in_hbm(queries), in_hbm(grad_out)),
        [dma((8,))],
        in_space=ANY,
    )
    query_slots = exchange(query_slots)
    own, own_late = call(
        functools.partial(order_keys, tok),
        "order_keys",
        [((2 * n * tok + EXTRA, HEAD), BF16), ((6 * tok + EXTRA, HEAD), BF16)],
        (info, *kv_slots),
        [pltpu.VMEM((EXTRA, HEAD), F32)],
    )
    near = ring(own, n)
    far = lax.ppermute(
        own_late, AXES, [(i, i + 2 * n if i + 2 * n < count else (i + 2 * n - count) ^ n) for i in range(count)]
    )
    blocks = 3 * n - 1
    results = call(
        functools.partial(attend, tok),
        "attend",
        [((2 * tok, GROUPS * HEAD), BF16)] * n
        + [((2 * n * tok, HEAD), F32), ((2 * n * tok, HEAD), BF16), ((6 * tok, HEAD), BF16)],
        (info, own, near, far, *query_slots),
        [
            pltpu.VMEM((blocks * tok, HEAD), BF16),
            pltpu.VMEM((blocks * tok, HEAD), BF16),
            pltpu.VMEM((24, tok), F32),
            pltpu.VMEM((blocks * tok, HEAD), F32),
            pltpu.VMEM((blocks * tok, HEAD), F32),
        ],
    )
    out_slots, (own_terms, near_terms, far_terms) = results[:n], results[n:]
    near_back = ring(near_terms, -n)
    far_back = ring(far_terms, -2 * n)
    out_slots = exchange(out_slots)
    grad_slots = call(
        functools.partial(add_terms, tok),
        "add_terms",
        [((2 * tok, HEAD), BF16)] * n,
        (info, own_terms, near_back, far_back),
        [pltpu.VMEM((2 * n * tok, HEAD), F32)],
    )
    grad_slots = exchange(grad_slots)
    attended, grad_queries = call(
        functools.partial(place_columns, tok, GROUPS * HEAD),
        "place_queries",
        [((tok, HEADS * HEAD), BF16)] * 2,
        (info, *out_slots),
        [dma((8,))],
        out_space=ANY,
    )
    grad_keys, grad_values = call(
        functools.partial(place_columns, tok, HEAD),
        "place_keys",
        [((tok, KV_HEADS * HEAD), BF16)] * 2,
        (info, *grad_slots),
        [dma((8,))],
        out_space=ANY,
    )
    return (attended, grad_queries, grad_keys, grad_values)


def solution(mesh):
    rows = P(AXES, None)
    return jax.shard_map(
        local,
        mesh=mesh,
        in_specs=(rows, rows, rows, rows, P(AXES)),
        out_specs=(rows, rows, rows, rows),
        check_vma=False,
    )
```
